32 devices in a mesh: groups: 2 (over x), gx: 2 (over core), gy: 8 (over z, y).
Axes of the slice: x: 2, y: 2, z: 4, core: 2. Of those that a mesh axis runs over, the one named last changes fastest.
Arguments:
- inputs: bfloat16 [24, 16384], P('groups', ('gx', 'gy')), parts along dimension 0, may hold values from -6 to 6
- norm_gain: bfloat16 [16384], P(('gx', 'gy')), may hold values from 0.099609375 to 1.8984375
- w_query: bfloat16 [16384, 8192], P('gx', 'gy'), may hold values from -0.046875 to 0.046875
- w_key: bfloat16 [16384, 512], P('gx', 'gy'), may hold values from -0.046875 to 0.046875
- w_value: bfloat16 [16384, 512], P('gx', 'gy'), may hold values from -0.046875 to 0.046875
- w_out: bfloat16 [8192, 16384], P('gy', 'gx'), may hold values from -0.25 to 0.25
- key_cache: bfloat16 [24, 16384, 128], P(('groups', 'gx'), 'gy'), parts along dimension 0, may hold values from -480 to 480
- value_cache: bfloat16 [24, 16384, 128], P(('groups', 'gx'), 'gy'), parts along dimension 0, may hold values from -6 to 6
- lengths: int32 [24], P(('groups', 'gx')), parts along dimension 0, may hold values from 1 to 4096, as said below
Outputs:
- output: bfloat16 [24, 16384], P('groups', ('gx', 'gy')), parts along dimension 0
The draws below stay inside these ranges and needn't reach their ends.
There are 2 independent parts, one for each index of `groups`. The reference program is written for one: setup_inputs(seed, part) draws one part's arguments, and reference() takes and returns one part's arrays. A program takes and returns all parts, laid end to end along the dimension named above; an argument that names none is the same for every part. Nothing has to cross between parts.
Inputs may be any that keep to these rules, and one draw needn't show every extreme that they name: `lengths`: one row has exactly 4096 cached tokens and another exactly 1.
All inputs are finite; a program needn't handle non-finite values.
Results may differ from the reference program's by a relative error of at most 0.017.
Values may be sent and summed in bfloat16 or wider, within the bound.
A program may use at most 128 MiB of HBM per device.

```python
import jax
import jax.numpy as jnp
from jax import lax

D = 16384
HQ = 64
KVH = 4
HD = 128
CTX = 4096
ROWS = 12


def draw_lengths(key, part):
    key = jax.random.fold_in(key, 11)
    key_exp, key_off, key_row, key_short = jax.random.split(key, 4)
    top_exp = max(CTX.bit_length() - 1, 1)
    exponents = jax.random.randint(key_exp, (ROWS,), 0, top_exp)
    lowest = jnp.left_shift(jnp.ones((ROWS,), jnp.int32), exponents)
    offsets = jax.random.randint(key_off, (ROWS,), 0, lowest)
    drawn = jnp.minimum(lowest + offsets, CTX)
    chosen = jax.random.randint(key_row, (), 0, ROWS)
    shorter = (chosen + 1 + jax.random.randint(key_short, (), 0, ROWS - 1)) % ROWS
    row_ids = jnp.arange(ROWS)
    drawn = jnp.where(row_ids == shorter, 1, drawn)
    return jnp.where(row_ids == chosen, CTX, drawn).astype(jnp.int32)


def draw_key_cache(key, part):
    key = jax.random.fold_in(key, 23)
    key_main = jax.random.fold_in(key, 0)
    base = jax.random.normal(key_main, (ROWS, KVH * CTX, HD), jnp.float32)
    values = jnp.clip(2.0 * base, -12.0, 12.0)
    return values.astype(jnp.bfloat16)


def levels(key, shape, cuts, smallest, top_value):
    gain = 1.0
    for dim, shards_of in cuts:
        draws = jax.random.uniform(jax.random.fold_in(jax.random.fold_in(key, 6), dim), (shards_of,), jnp.float32, smallest / len(cuts), top_value / len(cuts))
        gain = gain * jnp.repeat(jnp.exp(draws), shape[dim] // shards_of).reshape((-1,) + (1,) * (len(shape) - 1 - dim))
    return gain


def centred(rng, shape, scale, bound, shards=(), held_as=jnp.bfloat16):
    factor_of = levels(rng, shape, shards, -0.22, 0.18) if shards else 1.0
    array = jax.random.normal(rng, shape, jnp.float32) * scale * factor_of
    return jnp.minimum(jnp.maximum(array, -bound), bound).astype(held_as)


def setup_inputs(seed: int = 0, part: int = 0) -> dict:
    key_list = jax.random.split(jax.random.key(seed), 10)
    part_splits = jax.random.split(jax.random.fold_in(key_list[9], part), 10)
    return {
        "inputs": centred(part_splits[0], (ROWS, D), 1.0, 6.0, ((1, 16),)),
        "norm_gain": jnp.clip(1.0 + 0.18 * jax.random.normal(key_list[1], (D,), jnp.float32), 0.099609375, 1.8984375).astype(jnp.bfloat16),
        "w_query": centred(key_list[2], (D, HQ * HD), D ** -0.5, 0.046875, ((0, 2), (1, 8))),
        "w_key": centred(key_list[3], (D, KVH * HD), D ** -0.5, 0.046875, ((0, 2), (1, 8))),
        "w_value": centred(key_list[4], (D, KVH * HD), D ** -0.5, 0.046875, ((0, 2), (1, 8))),
        "w_out": centred(key_list[5], (HQ * HD, D), (HQ * HD // 16) ** -0.5, 0.25, ((0, 8), (1, 2))),
        "key_cache": draw_key_cache(jax.random.fold_in(jax.random.fold_in(key_list[9], part), 71), part),
        "value_cache": centred(part_splits[7], (ROWS, KVH * CTX, HD), 1.0, 6.0, ((0, 2), (1, 8))),
        "lengths": draw_lengths(jax.random.fold_in(jax.random.fold_in(key_list[9], part), 71), part),
    }


huge_score = 1e+30

def rotate(values, where_at):
    half_dim = values.shape[-1] // 2
    freq_index = jnp.arange(half_dim, dtype=jnp.float32)
    inverse = 500000.0 ** (-2.0 * freq_index / values.shape[-1])
    angles = where_at.astype(jnp.float32)[:, None] * inverse[None, :]
    cosine = jnp.cos(angles)[:, None, :]
    sine_part = jnp.sin(angles)[:, None, :]
    front_half = values[..., :half_dim]
    back_half = values[..., half_dim:]
    return jnp.concatenate([front_half * cosine - back_half * sine_part, back_half * cosine + front_half * sine_part], axis=-1)

def partial_attention(query_block, key_block, value_block, own_key, own_value, live_mask, with_self):
    score_scale = query_block.shape[-1] ** (-0.5)
    scores = jnp.einsum('rgd,rtd->rgt', query_block.astype(jnp.float32), key_block.astype(jnp.float32)) * score_scale
    self_score = lax.optimization_barrier(jnp.sum(query_block.astype(jnp.float32) * own_key.astype(jnp.float32)[:, None, :], axis=-1)) * score_scale
    masked = jnp.where(live_mask[:, None, :], scores, -huge_score)
    self_live = jnp.where(with_self, self_score, -huge_score)
    best_score = jnp.maximum(lax.optimization_barrier(jnp.max(masked, axis=-1)), self_live)
    exp_weights = jnp.where(live_mask[:, None, :], jnp.exp(masked - best_score[..., None]), 0.0)
    self_weight = jnp.where(with_self, jnp.exp(self_live - best_score), 0.0)
    denominator = lax.optimization_barrier(jnp.sum(exp_weights, axis=-1)) + self_weight
    weighted = jnp.einsum('rgt,rtd->rgd', exp_weights.astype(jnp.bfloat16).astype(jnp.float32), value_block.astype(jnp.float32))
    weighted = weighted + self_weight.astype(jnp.bfloat16).astype(jnp.float32)[..., None] * own_value.astype(jnp.float32)[:, None, :]
    return (best_score, denominator, weighted)

def reference(inputs, norm_gain, w_query, w_key, w_value, w_out, key_cache, value_cache, lengths):
    floats = inputs.astype(jnp.float32)
    scale_inv = lax.rsqrt(lax.optimization_barrier(jnp.mean(floats * floats, axis=-1, keepdims=True)) + 1e-05)
    normed = (floats * scale_inv * norm_gain.astype(jnp.float32)).astype(jnp.bfloat16)
    rows_all = inputs.shape[0]
    queries = jnp.dot(normed, w_query, preferred_element_type=jnp.float32).reshape(rows_all, HQ, HD)
    queries = rotate(queries, lengths).astype(jnp.bfloat16)
    new_keys = jnp.dot(normed, w_key, preferred_element_type=jnp.float32).reshape(rows_all, HD, KVH)
    new_keys = rotate(jnp.transpose(new_keys, (0, 2, 1)), lengths).astype(jnp.bfloat16)
    new_values = jnp.dot(normed, w_value, preferred_element_type=jnp.float32).reshape(rows_all, HD, KVH)
    new_values = jnp.transpose(new_values, (0, 2, 1)).astype(jnp.bfloat16)
    group_size = HQ // KVH
    grouped = queries.reshape(rows_all, group_size, KVH, HD)
    live_mask = jnp.arange(CTX, dtype=jnp.int32)[None, :] < lengths[:, None]

    def one_head(head_index):
        query_block = lax.dynamic_index_in_dim(grouped, head_index, 2, keepdims=False)
        key_block = lax.dynamic_slice_in_dim(key_cache, head_index * CTX, CTX, 1)
        value_block = lax.dynamic_slice_in_dim(value_cache, head_index * CTX, CTX, 1)
        own_key = lax.dynamic_index_in_dim(new_keys, head_index, 1, keepdims=False)
        own_value = lax.dynamic_index_in_dim(new_values, head_index, 1, keepdims=False)
        best_score, denominator, weighted = partial_attention(query_block, key_block, value_block, own_key, own_value, live_mask, True)
        return weighted / denominator[..., None]
    results = lax.map(one_head, jnp.arange(KVH, dtype=jnp.int32))
    attended = jnp.transpose(results, (1, 2, 0, 3)).reshape(rows_all, HQ * HD).astype(jnp.bfloat16)
    return jnp.dot(attended, w_out, preferred_element_type=jnp.float32).astype(jnp.bfloat16)
```

```python
import functools

import jax
import jax.numpy as jnp
from jax import lax
from jax.experimental import pallas as pl
from jax.experimental.pallas import tpu as pltpu
from jax.sharding import PartitionSpec as P

KVH = 4
HD = 128
SUB = 8
HUGE = 1e30
MESH = pl.DeviceIdType.MESH


def rope_table(lengths):
    half_dim = HD // 2
    freq_index = jnp.arange(half_dim, dtype=jnp.float32)
    inverse = 500000.0 ** (-2.0 * freq_index / HD)
    floats = lengths.astype(jnp.float32)
    angles = floats[:, None] * inverse[None, :]
    cosine, sine = jnp.cos(angles), jnp.sin(angles)
    table = jnp.stack(
        [
            jnp.concatenate([cosine, cosine], axis=1),
            jnp.concatenate([-sine, sine], axis=1),
            jnp.broadcast_to(floats[:, None], (lengths.shape[0], HD)),
        ]
    )
    return jnp.pad(table, ((0, 0), (0, SUB - lengths.shape[0]), (0, 0)))


def block_kernel(
    gy, gx_count, rows,
    table, xp, wq, wk, wv, wo, kc, vc,
    out,
    xall, ssq, wq_v, wk_v, wv_v, wo_v, kc_v, vc_v,
    part, kpart, vpart, part_in, qsend, qin, qg, outbox, inbox, att, osend, oin,
    sem_wq, sem_wk, sem_wv, sem_wo, sem_kc, sem_vc,
    ssq_s, ssq_r, x_s, x_r, part_s, part_r, q_s, q_r, box_s, box_r, att_s, att_r, o_s, o_r,
):
    gx = lax.axis_index("gx")
    me = lax.axis_index("gy")
    other = 1 - gx
    bd = xp.shape[1]
    qw = wq.shape[1]
    ck = wk.shape[1]
    span = kc.shape[1]
    ow = wo.shape[1] // gy
    hh = qw // HD
    hq = max(1, hh // KVH)
    nq = gy * hh // KVH
    bph = gy // KVH
    group = me // bph
    block = me % bph
    d_model = bd * gy * gx_count

    def load_in(step):
        base = pl.multiple_of(((me + step) % gy) * bd, bd)
        rows_here = pl.ds(base, bd)
        return (
            pltpu.make_async_copy(wq.at[rows_here, :], wq_v.at[step], sem_wq.at[step]),
            pltpu.make_async_copy(wk.at[rows_here, :], wk_v.at[step], sem_wk.at[step]),
            pltpu.make_async_copy(wv.at[rows_here, :], wv_v.at[step], sem_wv.at[step]),
        )

    def load_out(step):
        base = pl.multiple_of(((me + step) % gy) * ow, ow)
        return pltpu.make_async_copy(wo.at[:, pl.ds(base, ow)], wo_v.at[step], sem_wo.at[step])

    def load_cache(row):
        return (
            pltpu.make_async_copy(kc.at[row], kc_v.at[row], sem_kc.at[row]),
            pltpu.make_async_copy(vc.at[row], vc_v.at[row], sem_vc.at[row]),
        )

    for step in range(gy):
        for copy in load_in(step):
            copy.start()

    barrier = pltpu.get_barrier_semaphore()
    for side in range(gx_count):
        for step in range(gy):
            if side == 0 and step == 0:
                continue
            pl.semaphore_signal(
                barrier, inc=1,
                device_id={"gx": (gx + side) % gx_count, "gy": (me + step) % gy},
                device_id_type=MESH,
            )

    mine = xp[...].astype(jnp.float32)
    diagonal = lax.broadcasted_iota(jnp.int32, (2 * SUB, HD), 0) == lax.broadcasted_iota(
        jnp.int32, (2 * SUB, HD), 1
    )
    squares = jnp.sum(mine * mine, axis=1, keepdims=True)
    my_id = gx * gy + me
    ssq[my_id] = jnp.broadcast_to(
        jnp.sum(jnp.where(diagonal, squares, 0.0), axis=0, keepdims=True), (SUB, HD)
    )
    xall[me] = xp[...]

    pl.semaphore_wait(barrier, gx_count * gy - 1)

    def ssq_copy(side, step, source):
        return pltpu.make_async_remote_copy(
            src_ref=ssq.at[my_id, pl.ds(0, 1)], dst_ref=ssq.at[source, pl.ds(0, 1)],
            send_sem=ssq_s.at[side, step], recv_sem=ssq_r.at[source],
            device_id={"gx": (gx + side) % gx_count, "gy": (me + step) % gy},
            device_id_type=MESH,
        )

    def peer_copy(src, dst, send, recv, step):
        return pltpu.make_async_remote_copy(
            src_ref=src, dst_ref=dst, send_sem=send, recv_sem=recv,
            device_id={"gy": (me + step) % gy}, device_id_type=MESH,
        )

    def core_copy(src, dst, send, recv):
        return pltpu.make_async_remote_copy(
            src_ref=src, dst_ref=dst, send_sem=send, recv_sem=recv,
            device_id={"gx": other}, device_id_type=MESH,
        )

    def x_copy(step, source):
        return peer_copy(xp, xall.at[source], x_s.at[step], x_r.at[source], step)

    for side in range(gx_count):
        for step in range(gy):
            if side or step:
                ssq_copy(side, step, my_id).start()
    for step in range(1, gy):
        x_copy(step, me).start()
    for row in range(rows):
        for copy in load_cache(row):
            copy.start()

    part[...] = jnp.zeros_like(part)
    kpart[...] = jnp.zeros_like(kpart)
    vpart[...] = jnp.zeros_like(vpart)
    outbox[...] = jnp.zeros_like(outbox)

    for side in range(gx_count):
        for step in range(gy):
            if side or step:
                source = ((gx + side) % gx_count) * gy + (me + step) % gy
                ssq_copy(side, step, source).wait_recv()
    total = jnp.sum(ssq[:, 0, :], axis=0, keepdims=True)
    total = jnp.sum(jnp.where(diagonal, total, 0.0), axis=1, keepdims=True)
    scale_inv = lax.rsqrt(total / d_model + 1e-05)

    def project(step):
        source = (me + step) % gy
        features = xall[source].astype(jnp.float32)
        gain = features[rows : rows + 1, :]
        normed = (features * scale_inv * gain).astype(jnp.bfloat16)
        for copy in load_in(step):
            copy.wait()
        query = jnp.dot(normed, wq_v[step], preferred_element_type=jnp.float32)
        part[0, :, :qw] += query[:SUB]
        part[1, :, :qw] += query[SUB:]
        kpart[...] += jnp.dot(normed, wk_v[step], preferred_element_type=jnp.float32)
        vpart[...] += jnp.dot(normed, wv_v[step], preferred_element_type=jnp.float32)

    project(0)

    @pl.loop(1, gy)
    def _(step):
        source = (me + step) % gy
        x_copy(step, source).wait_recv()
        project(step)

    for side in range(2):
        part[side, :, qw : qw + ck] = kpart[side * SUB : (side + 1) * SUB]
        part[side, :, qw + HD : qw + HD + ck] = vpart[side * SUB : (side + 1) * SUB]

    swap = core_copy(part.at[other], part_in, part_s, part_r)
    swap.start()
    for step in range(gy):
        load_out((step + 1) % gy).start()
    column = lax.broadcasted_iota(jnp.int32, (HD, KVH * HD), 0)
    target = lax.broadcasted_iota(jnp.int32, (HD, KVH * HD), 1)
    wanted = (target % HD) * KVH + target // HD
    select = jnp.where((column < ck) & (column + me * ck == wanted), 1.0, 0.0).astype(jnp.bfloat16)
    cosine, sine, lens = table[0], table[1], table[2]
    swap.wait_recv()

    def rotated(values):
        return values * cosine + pltpu.roll(values, HD // 2, 1) * sine

    summed = part[gx] + part_in[...]
    for slot in range(hh):
        turned = rotated(summed[:, slot * HD : (slot + 1) * HD])
        to_group = slot % KVH if hh % KVH == 0 else (me * hh + slot) % KVH
        qsend[to_group, slot // KVH] = turned.astype(jnp.bfloat16).astype(jnp.float32)
    pair = jnp.concatenate([summed[:, qw : qw + HD], summed[:, qw + HD :]], axis=0)
    high = pair.astype(jnp.bfloat16)
    rest = pair - high.astype(jnp.float32)
    middle = rest.astype(jnp.bfloat16)
    low = (rest - middle.astype(jnp.float32)).astype(jnp.bfloat16)
    placed = (
        jnp.dot(high, select, preferred_element_type=jnp.float32)
        + jnp.dot(middle, select, preferred_element_type=jnp.float32)
        + jnp.dot(low, select, preferred_element_type=jnp.float32)
    )
    for g in range(KVH):
        qsend[g, hq] = placed[:SUB, g * HD : (g + 1) * HD]
        qsend[g, hq + 1] = placed[SUB:, g * HD : (g + 1) * HD]

    def q_copy(step, source):
        return peer_copy(
            qsend.at[((me + step) % gy) // bph], qin.at[source],
            q_s.at[step], q_r.at[source], step,
        )

    for step in range(1, gy):
        q_copy(step, me).start()
    qin[me] = qsend[group]
    for step in range(1, gy):
        q_copy(step, (me + step) % gy).wait_recv()

    for n in range(nq):
        if hh % KVH == 0:
            qg[n] = qin[n * KVH // hh, (n * KVH % hh) // KVH]
        else:
            qg[n] = qin[(n * KVH + group) // hh, 0]
    own_key = rotated(jnp.sum(qin[:, hq], axis=0)).astype(jnp.bfloat16).astype(jnp.float32)
    own_value = jnp.sum(qin[:, hq + 1], axis=0).astype(jnp.bfloat16).astype(jnp.float32)

    score_scale = HD ** (-0.5)
    with_self = (lax.broadcasted_iota(jnp.int32, (nq, 1), 0) * 0 + block) == 0
    positions = (lax.broadcasted_iota(jnp.int32, (nq, span), 1) + block * span).astype(jnp.float32)
    lane = lax.broadcasted_iota(jnp.int32, (nq, HD), 1)
    for row in range(rows):
        for copy in load_cache(row):
            copy.wait()
        query = qg[:, row, :]
        scores = (
            lax.dot_general(
                query.astype(jnp.bfloat16), kc_v[row], (((1,), (1,)), ((), ())),
                preferred_element_type=jnp.float32,
            )
            * score_scale
        )
        live = positions < lens[row : row + 1, 0:1]
        masked = jnp.where(live, scores, -HUGE)
        self_score = (
            jnp.sum(query * own_key[row : row + 1, :], axis=1, keepdims=True) * score_scale
        )
        self_live = jnp.where(with_self, self_score, -HUGE)
        best = jnp.maximum(jnp.max(masked, axis=1, keepdims=True), self_live)
        weights = jnp.where(live, jnp.exp(masked - best), 0.0)
        self_weight = jnp.where(with_self, jnp.exp(self_live - best), 0.0)
        denominator = jnp.sum(weights, axis=1, keepdims=True) + self_weight
        weighted = jnp.dot(
            weights.astype(jnp.bfloat16), vc_v[row], preferred_element_type=jnp.float32
        )
        weighted = (
            weighted
            + self_weight.astype(jnp.bfloat16).astype(jnp.float32) * own_value[row : row + 1, :]
        )
        outbox[:, 0, row, :] = weighted
        outbox[:, 1, row, :] = jnp.where(lane < HD // 2, best, denominator)

    def box_copy(step, source):
        first = (((me + step) % gy) * hh) // KVH
        return peer_copy(
            outbox.at[pl.ds(first, hq)], inbox.at[source], box_s.at[step], box_r.at[source], step
        )

    for step in range(1, gy):
        box_copy(step, me).start()
    inbox[me] = outbox[pl.ds((me * hh) // KVH, hq)]
    for step in range(1, gy):
        box_copy(step, (me + step) % gy).wait_recv()

    for slot in range(hh):
        of_group = slot % KVH if hh % KVH == 0 else (me * hh + slot) % KVH
        sums = [inbox[of_group * bph + b, slot // KVH, 0] for b in range(bph)]
        stats = [inbox[of_group * bph + b, slot // KVH, 1] for b in range(bph)]
        bests = [s[:, 0:1] for s in stats]
        denominators = [s[:, HD // 2 : HD // 2 + 1] for s in stats]
        overall = functools.reduce(jnp.maximum, bests)
        factors = [jnp.exp(b - overall) for b in bests]
        denominator = sum(f * d for f, d in zip(factors, denominators))
        weighted = sum(f * s for f, s in zip(factors, sums))
        att[gx, :, slot * HD : (slot + 1) * HD] = (
            (weighted / denominator).astype(jnp.bfloat16).astype(jnp.float32)
        )

    att_swap = core_copy(att.at[gx], att.at[gx], att_s, att_r)
    att_swap.start()
    core_copy(att.at[other], att.at[other], att_s, att_r).wait_recv()
    attended = jnp.concatenate([att[0], att[1]], axis=0).astype(jnp.bfloat16)

    def o_copy(step, source):
        return peer_copy(osend.at[step], oin.at[source], o_s.at[step], o_r.at[source], step)

    @pl.loop(1, gy)
    def _(step):
        load_out(step).wait()
        osend[step] = jnp.dot(
            attended, wo_v[step], preferred_element_type=jnp.float32
        ).astype(jnp.bfloat16)
        o_copy(step, me).start()

    load_out(0).wait()
    result = jnp.dot(attended, wo_v[0], preferred_element_type=jnp.float32)
    for step in range(1, gy):
        source = (me + step) % gy
        o_copy(step, source).wait_recv()
        result = result + oin[source].astype(jnp.float32)
    out[...] = result.astype(out.dtype)

    swap.wait_send()
    att_swap.wait_send()
    for side in range(gx_count):
        for step in range(gy):
            if side or step:
                ssq_copy(side, step, my_id).wait_send()
    for step in range(1, gy):
        x_copy(step, me).wait_send()
        q_copy(step, me).wait_send()
        box_copy(step, me).wait_send()
        o_copy(step, me).wait_send()


def local(inputs, norm_gain, w_query, w_key, w_value, w_out, key_cache, value_cache, lengths):
    gy, gx_count = lax.axis_size("gy"), lax.axis_size("gx")
    rows, span, _ = key_cache.shape
    bd = inputs.shape[1]
    qw, ck = w_query.shape[1], w_key.shape[1]
    ow = w_out.shape[1] // gy
    hh = qw // HD
    hq = max(1, hh // KVH)
    nq = gy * hh // KVH
    bf16, f32 = jnp.bfloat16, jnp.float32

    gap = jnp.zeros((SUB - rows - 1, bd), bf16)
    end = jnp.zeros((SUB - rows, bd), bf16)
    packed = jnp.concatenate([inputs[:rows], norm_gain[None, :], gap, inputs[rows:], end], axis=0)

    vmem = pl.BlockSpec(memory_space=pltpu.VMEM)
    hbm = pl.BlockSpec(memory_space=pl.ANY)
    dma = pltpu.SemaphoreType.DMA
    scratch = [
        pltpu.VMEM((gy, 2 * SUB, bd), bf16),
        pltpu.VMEM((gx_count * gy, SUB, HD), f32),
        pltpu.VMEM((gy, bd, qw), bf16),
        pltpu.VMEM((gy, bd, ck), bf16),
        pltpu.VMEM((gy, bd, ck), bf16),
        pltpu.VMEM((gy, w_out.shape[0], ow), bf16),
        pltpu.VMEM(key_cache.shape, bf16),
        pltpu.VMEM(value_cache.shape, bf16),
        pltpu.VMEM((2, SUB, qw + 2 * HD), f32),
        pltpu.VMEM((2 * SUB, ck), f32),
        pltpu.VMEM((2 * SUB, ck), f32),
        pltpu.VMEM((SUB, qw + 2 * HD), f32),
        pltpu.VMEM((KVH, hq + 2, SUB, HD), f32),
        pltpu.VMEM((gy, hq + 2, SUB, HD), f32),
        pltpu.VMEM((nq, SUB, HD), f32),
        pltpu.VMEM((nq, 2, SUB, HD), f32),
        pltpu.VMEM((gy, hq, 2, SUB, HD), f32),
        pltpu.VMEM((2, SUB, qw), f32),
        pltpu.VMEM((gy, 2 * SUB, ow), bf16),
        pltpu.VMEM((gy, 2 * SUB, ow), bf16),
        dma((gy,)), dma((gy,)), dma((gy,)), dma((gy,)), dma((rows,)), dma((rows,)),
        dma((gx_count, gy)), dma((gx_count * gy,)),
        dma((gy,)), dma((gy,)),
        dma, dma,
        dma((gy,)), dma((gy,)),
        dma((gy,)), dma((gy,)),
        dma, dma,
        dma((gy,)), dma((gy,)),
    ]
    result = pl.pallas_call(
        functools.partial(block_kernel, gy, gx_count, rows),
        out_shape=jax.ShapeDtypeStruct((2 * SUB, ow), bf16),
        in_specs=[vmem, vmem] + [hbm] * 6,
        out_specs=vmem,
        scratch_shapes=scratch,
        compiler_params=pltpu.CompilerParams(
            collective_id=0, has_side_effects=True, vmem_limit_bytes=52 * 2**20
        ),
    )(rope_table(lengths), packed, w_query, w_key, w_value, w_out, key_cache, value_cache)
    return jnp.concatenate([result[:rows], result[SUB : SUB + rows]], axis=0)


def solution(mesh):
    placed = (
        P("groups", ("gx", "gy")),
        P(("gx", "gy")),
        P("gx", "gy"),
        P("gx", "gy"),
        P("gx", "gy"),
        P("gy", "gx"),
        P(("groups", "gx"), "gy", None),
        P(("groups", "gx"), "gy", None),
        P(("groups", "gx")),
    )
    return jax.shard_map(
        local, mesh=mesh, in_specs=placed, out_specs=P("groups", ("gx", "gy")), check_vma=False
    )
```

```python
import functools

import jax
import jax.numpy as jnp
import numpy as np
from jax import lax
from jax.experimental import pallas as pl
from jax.experimental.pallas import tpu as pltpu
from jax.sharding import PartitionSpec as P

KVH = 4
HD = 128
SUB = 8
HUGE = 1e30
MESH = pl.DeviceIdType.MESH


def block_kernel(
    gy, gx_count, rows,
    lengths, inverse, x, gain, wq, wk, wv, wo, kc, vc,
    out,
    xall, ssq, wq_v, wk_v, wv_v, wo_v, kc_v, vc_v,
    part, kpart, vpart, part_in, qsend, qin, qg, outbox, inbox, att, osend, oin,
    sem_wq, sem_wk, sem_wv, sem_wo, sem_kc, sem_vc,
    ssq_s, ssq_r, x_s, x_r, part_s, part_r, q_s, q_r, box_s, box_r, att_s, att_r, o_s, o_r,
):
    gx = lax.axis_index("gx")
    me = lax.axis_index("gy")
    other = 1 - gx
    bd = x.shape[1]
    qw = wq.shape[1]
    ck = wk.shape[0]
    span = kc.shape[1]
    ow = wo.shape[1] // gy
    hh = qw // HD
    hq = max(1, hh // KVH)
    nq = gy * hh // KVH
    bph = gy // KVH
    group = me // bph
    block = me % bph
    d_model = bd * gy * gx_count

    def load_in(step):
        base = pl.multiple_of(((me + step) % gy) * bd, bd)
        rows_here = pl.ds(base, bd)
        return (
            pltpu.make_async_copy(wq.at[rows_here, :], wq_v.at[step], sem_wq.at[step]),
            pltpu.make_async_copy(wk.at[:, rows_here], wk_v.at[step], sem_wk.at[step]),
            pltpu.make_async_copy(wv.at[:, rows_here], wv_v.at[step], sem_wv.at[step]),
        )

    def load_out(step):
        base = pl.multiple_of(((me + step) % gy) * ow, ow)
        return pltpu.make_async_copy(wo.at[:, pl.ds(base, ow)], wo_v.at[step], sem_wo.at[step])

    def load_cache(row):
        return (
            pltpu.make_async_copy(kc.at[row], kc_v.at[row], sem_kc.at[row]),
            pltpu.make_async_copy(vc.at[row], vc_v.at[row], sem_vc.at[row]),
        )

    for step in range(gy):
        for copy in load_in(step):
            copy.start()

    barrier = pltpu.get_barrier_semaphore()
    for side in range(gx_count):
        for step in range(gy):
            if side == 0 and step == 0:
                continue
            pl.semaphore_signal(
                barrier, inc=1,
                device_id={"gx": (gx + side) % gx_count, "gy": (me + step) % gy},
                device_id_type=MESH,
            )

    own = x[...].astype(jnp.float32)
    mine = jnp.concatenate(
        [
            own[:rows], gain[...].astype(jnp.float32), jnp.zeros((SUB - rows - 1, bd), jnp.float32),
            own[rows:], jnp.zeros((SUB - rows, bd), jnp.float32),
        ],
        axis=0,
    )
    diagonal = lax.broadcasted_iota(jnp.int32, (2 * SUB, HD), 0) == lax.broadcasted_iota(
        jnp.int32, (2 * SUB, HD), 1
    )
    squares = jnp.sum(mine * mine, axis=1, keepdims=True)
    my_id = gx * gy + me
    ssq[my_id] = jnp.broadcast_to(
        jnp.sum(jnp.where(diagonal, squares, 0.0), axis=0, keepdims=True), (SUB, HD)
    )
    xall[me] = mine.astype(jnp.bfloat16)

    pl.semaphore_wait(barrier, gx_count * gy - 1)

    def ssq_copy(side, step, source):
        return pltpu.make_async_remote_copy(
            src_ref=ssq.at[my_id, pl.ds(0, 1)], dst_ref=ssq.at[source, pl.ds(0, 1)],
            send_sem=ssq_s.at[side, step], recv_sem=ssq_r.at[source],
            device_id={"gx": (gx + side) % gx_count, "gy": (me + step) % gy},
            device_id_type=MESH,
        )

    def peer_copy(src, dst, send, recv, step):
        return pltpu.make_async_remote_copy(
            src_ref=src, dst_ref=dst, send_sem=send, recv_sem=recv,
            device_id={"gy": (me + step) % gy}, device_id_type=MESH,
        )

    def core_copy(src, dst, send, recv):
        return pltpu.make_async_remote_copy(
            src_ref=src, dst_ref=dst, send_sem=send, recv_sem=recv,
            device_id={"gx": other}, device_id_type=MESH,
        )

    def x_copy(step, source):
        return peer_copy(xall.at[me], xall.at[source], x_s.at[step], x_r.at[source], step)

    for side in range(gx_count):
        for step in range(gy):
            if side or step:
                ssq_copy(side, step, my_id).start()
    for step in range(1, gy):
        x_copy(step, me).start()
    for row in range(rows):
        for copy in load_cache(row):
            copy.start()

    part[...] = jnp.zeros_like(part)
    kpart[...] = jnp.zeros_like(kpart)
    vpart[...] = jnp.zeros_like(vpart)
    row_of = lax.broadcasted_iota(jnp.int32, (SUB, HD), 0)
    lens = jnp.zeros((SUB, HD), jnp.int32)
    for row in range(rows):
        lens = jnp.where(row_of == row, lengths[row], lens)
    lens = lens.astype(jnp.float32)
    angles = lens * inverse[...]
    cosine = jnp.cos(angles)
    sine = jnp.sin(angles)
    sine = jnp.where(lax.broadcasted_iota(jnp.int32, (SUB, HD), 1) < HD // 2, -sine, sine)
    outbox[...] = jnp.zeros_like(outbox)

    for side in range(gx_count):
        for step in range(gy):
            if side or step:
                source = ((gx + side) % gx_count) * gy + (me + step) % gy
                ssq_copy(side, step, source).wait_recv()
    total = jnp.sum(ssq[:, 0, :], axis=0, keepdims=True)
    total = jnp.sum(jnp.where(diagonal, total, 0.0), axis=1, keepdims=True)
    scale_inv = lax.rsqrt(total / d_model + 1e-05)

    def project(step):
        source = (me + step) % gy
        features = xall[source].astype(jnp.float32)
        gain = features[rows : rows + 1, :]
        normed = (features * scale_inv * gain).astype(jnp.bfloat16)
        for copy in load_in(step):
            copy.wait()
        query = jnp.dot(normed, wq_v[step], preferred_element_type=jnp.float32)
        part[0, :, :qw] += query[:SUB]
        part[1, :, :qw] += query[SUB:]
        across = (((1,), (1,)), ((), ()))
        kpart[...] += lax.dot_general(
            normed, wk_v[step], across, preferred_element_type=jnp.float32
        )
        vpart[...] += lax.dot_general(
            normed, wv_v[step], across, preferred_element_type=jnp.float32
        )

    project(0)

    @pl.loop(1, gy)
    def _(step):
        source = (me + step) % gy
        x_copy(step, source).wait_recv()
        project(step)

    for side in range(2):
        part[side, :, qw : qw + ck] = kpart[side * SUB : (side + 1) * SUB]
        part[side, :, qw + HD : qw + HD + ck] = vpart[side * SUB : (side + 1) * SUB]

    swap = core_copy(part.at[other], part_in, part_s, part_r)
    swap.start()
    for step in range(gy):
        load_out((step + 1) % gy).start()
    column = lax.broadcasted_iota(jnp.int32, (HD, KVH * HD), 0)
    target = lax.broadcasted_iota(jnp.int32, (HD, KVH * HD), 1)
    wanted = (target % HD) * KVH + target // HD
    select = jnp.where((column < ck) & (column + me * ck == wanted), 1.0, 0.0).astype(jnp.bfloat16)
    swap.wait_recv()

    def rotated(values):
        return values * cosine + pltpu.roll(values, HD // 2, 1) * sine

    summed = part[gx] + part_in[...]
    for slot in range(hh):
        turned = rotated(summed[:, slot * HD : (slot + 1) * HD])
        to_group = slot % KVH if hh % KVH == 0 else (me * hh + slot) % KVH
        qsend[to_group, slot // KVH] = turned.astype(jnp.bfloat16).astype(jnp.float32)
    pair = jnp.concatenate([summed[:, qw : qw + HD], summed[:, qw + HD :]], axis=0)
    high = pair.astype(jnp.bfloat16)
    rest = pair - high.astype(jnp.float32)
    middle = rest.astype(jnp.bfloat16)
    low = (rest - middle.astype(jnp.float32)).astype(jnp.bfloat16)
    placed = (
        jnp.dot(high, select, preferred_element_type=jnp.float32)
        + jnp.dot(middle, select, preferred_element_type=jnp.float32)
        + jnp.dot(low, select, preferred_element_type=jnp.float32)
    )
    for g in range(KVH):
        qsend[g, hq] = placed[:SUB, g * HD : (g + 1) * HD]
        qsend[g, hq + 1] = placed[SUB:, g * HD : (g + 1) * HD]

    def q_copy(step, source):
        return peer_copy(
            qsend.at[((me + step) % gy) // bph], qin.at[source],
            q_s.at[step], q_r.at[source], step,
        )

    for step in range(1, gy):
        q_copy(step, me).start()
    qin[me] = qsend[group]
    for step in range(1, gy):
        q_copy(step, (me + step) % gy).wait_recv()

    for n in range(nq):
        if hh % KVH == 0:
            qg[n] = qin[n * KVH // hh, (n * KVH % hh) // KVH]
        else:
            qg[n] = qin[(n * KVH + group) // hh, 0]
    own_key = rotated(jnp.sum(qin[:, hq], axis=0)).astype(jnp.bfloat16).astype(jnp.float32)
    own_value = jnp.sum(qin[:, hq + 1], axis=0).astype(jnp.bfloat16).astype(jnp.float32)

    score_scale = HD ** (-0.5)
    with_self = (lax.broadcasted_iota(jnp.int32, (nq, 1), 0) * 0 + block) == 0
    positions = (lax.broadcasted_iota(jnp.int32, (nq, span), 1) + block * span).astype(jnp.float32)
    lane = lax.broadcasted_iota(jnp.int32, (nq, HD), 1)
    for row in range(rows):
        for copy in load_cache(row):
            copy.wait()
        query = qg[:, row, :]
        scores = (
            lax.dot_general(
                query.astype(jnp.bfloat16), kc_v[row], (((1,), (1,)), ((), ())),
                preferred_element_type=jnp.float32,
            )
            * score_scale
        )
        live = positions < lens[row : row + 1, 0:1]
        masked = jnp.where(live, scores, -HUGE)
        self_score = (
            jnp.sum(query * own_key[row : row + 1, :], axis=1, keepdims=True) * score_scale
        )
        self_live = jnp.where(with_self, self_score, -HUGE)
        best = jnp.maximum(jnp.max(masked, axis=1, keepdims=True), self_live)
        weights = jnp.where(live, jnp.exp(masked - best), 0.0)
        self_weight = jnp.where(with_self, jnp.exp(self_live - best), 0.0)
        denominator = jnp.sum(weights, axis=1, keepdims=True) + self_weight
        weighted = jnp.dot(
            weights.astype(jnp.bfloat16), vc_v[row], preferred_element_type=jnp.float32
        )
        weighted = (
            weighted
            + self_weight.astype(jnp.bfloat16).astype(jnp.float32) * own_value[row : row + 1, :]
        )
        outbox[:, 0, row, :] = weighted
        outbox[:, 1, row, :] = jnp.where(lane < HD // 2, best, denominator)

    def box_copy(step, source):
        first = (((me + step) % gy) * hh) // KVH
        return peer_copy(
            outbox.at[pl.ds(first, hq)], inbox.at[source], box_s.at[step], box_r.at[source], step
        )

    for step in range(1, gy):
        box_copy(step, me).start()
    inbox[me] = outbox[pl.ds((me * hh) // KVH, hq)]
    for step in range(1, gy):
        box_copy(step, (me + step) % gy).wait_recv()

    for slot in range(hh):
        of_group = slot % KVH if hh % KVH == 0 else (me * hh + slot) % KVH
        sums = [inbox[of_group * bph + b, slot // KVH, 0] for b in range(bph)]
        stats = [inbox[of_group * bph + b, slot // KVH, 1] for b in range(bph)]
        bests = [s[:, 0:1] for s in stats]
        denominators = [s[:, HD // 2 : HD // 2 + 1] for s in stats]
        overall = functools.reduce(jnp.maximum, bests)
        factors = [jnp.exp(b - overall) for b in bests]
        denominator = sum(f * d for f, d in zip(factors, denominators))
        weighted = sum(f * s for f, s in zip(factors, sums))
        att[gx, :, slot * HD : (slot + 1) * HD] = (
            (weighted / denominator).astype(jnp.bfloat16).astype(jnp.float32)
        )

    att_swap = core_copy(att.at[gx], att.at[gx], att_s, att_r)
    att_swap.start()
    core_copy(att.at[other], att.at[other], att_s, att_r).wait_recv()
    attended = jnp.concatenate([att[0], att[1]], axis=0).astype(jnp.bfloat16)

    def o_copy(step, source):
        return peer_copy(osend.at[step], oin.at[source], o_s.at[step], o_r.at[source], step)

    @pl.loop(1, gy)
    def _(step):
        load_out(step).wait()
        osend[step] = jnp.dot(
            attended, wo_v[step], preferred_element_type=jnp.float32
        ).astype(jnp.bfloat16)
        o_copy(step, me).start()

    load_out(0).wait()
    result = jnp.dot(attended, wo_v[0], preferred_element_type=jnp.float32)
    for step in range(1, gy):
        source = (me + step) % gy
        o_copy(step, source).wait_recv()
        result = result + oin[source].astype(jnp.float32)
    out[...] = result.astype(out.dtype)

    swap.wait_send()
    att_swap.wait_send()
    for side in range(gx_count):
        for step in range(gy):
            if side or step:
                ssq_copy(side, step, my_id).wait_send()
    for step in range(1, gy):
        x_copy(step, me).wait_send()
        q_copy(step, me).wait_send()
        box_copy(step, me).wait_send()
        o_copy(step, me).wait_send()


def local(inputs, norm_gain, w_query, w_key, w_value, w_out, key_cache, value_cache, lengths):
    gy, gx_count = lax.axis_size("gy"), lax.axis_size("gx")
    rows, span, _ = key_cache.shape
    bd = inputs.shape[1]
    qw, ck = w_query.shape[1], w_key.shape[1]
    ow = w_out.shape[1] // gy
    hh = qw // HD
    hq = max(1, hh // KVH)
    nq = gy * hh // KVH
    bf16, f32 = jnp.bfloat16, jnp.float32

    half_dim = HD // 2
    inverse = 500000.0 ** (-2.0 * np.arange(half_dim, dtype=np.float64) / HD)
    inverse = jnp.asarray(np.tile(inverse, 2)[None, :], f32)

    vmem = pl.BlockSpec(memory_space=pltpu.VMEM)
    hbm = pl.BlockSpec(memory_space=pl.ANY)
    dma = pltpu.SemaphoreType.DMA
    scratch = [
        pltpu.VMEM((gy, 2 * SUB, bd), bf16),
        pltpu.VMEM((gx_count * gy, SUB, HD), f32),
        pltpu.VMEM((gy, bd, qw), bf16),
        pltpu.VMEM((gy, ck, bd), bf16),
        pltpu.VMEM((gy, ck, bd), bf16),
        pltpu.VMEM((gy, w_out.shape[0], ow), bf16),
        pltpu.VMEM(key_cache.shape, bf16),
        pltpu.VMEM(value_cache.shape, bf16),
        pltpu.VMEM((2, SUB, qw + 2 * HD), f32),
        pltpu.VMEM((2 * SUB, ck), f32),
        pltpu.VMEM((2 * SUB, ck), f32),
        pltpu.VMEM((SUB, qw + 2 * HD), f32),
        pltpu.VMEM((KVH, hq + 2, SUB, HD), f32),
        pltpu.VMEM((gy, hq + 2, SUB, HD), f32),
        pltpu.VMEM((nq, SUB, HD), f32),
        pltpu.VMEM((nq, 2, SUB, HD), f32),
        pltpu.VMEM((gy, hq, 2, SUB, HD), f32),
        pltpu.VMEM((2, SUB, qw), f32),
        pltpu.VMEM((gy, 2 * SUB, ow), bf16),
        pltpu.VMEM((gy, 2 * SUB, ow), bf16),
        dma((gy,)), dma((gy,)), dma((gy,)), dma((gy,)), dma((rows,)), dma((rows,)),
        dma((gx_count, gy)), dma((gx_count * gy,)),
        dma((gy,)), dma((gy,)),
        dma, dma,
        dma((gy,)), dma((gy,)),
        dma((gy,)), dma((gy,)),
        dma, dma,
        dma((gy,)), dma((gy,)),
    ]
    result = pl.pallas_call(
        functools.partial(block_kernel, gy, gx_count, rows),
        out_shape=jax.ShapeDtypeStruct((2 * SUB, ow), bf16),
        in_specs=[pl.BlockSpec(memory_space=pltpu.SMEM)] + [vmem] * 3 + [hbm] * 6,
        out_specs=vmem,
        scratch_shapes=scratch,
        compiler_params=pltpu.CompilerParams(
            collective_id=0, has_side_effects=True, vmem_limit_bytes=60 * 2**20
        ),
    )(
        lengths, inverse, inputs, norm_gain[None, :],
        w_query, w_key.T, w_value.T, w_out, key_cache, value_cache,
    )
    return jnp.concatenate([result[:rows], result[SUB : SUB + rows]], axis=0)


def solution(mesh):
    placed = (
        P("groups", ("gx", "gy")),
        P(("gx", "gy")),
        P("gx", "gy"),
        P("gx", "gy"),
        P("gx", "gy"),
        P("gy", "gx"),
        P(("groups", "gx"), "gy", None),
        P(("groups", "gx"), "gy", None),
        P(("groups", "gx")),
    )
    return jax.shard_map(
        local, mesh=mesh, in_specs=placed, out_specs=P("groups", ("gx", "gy")), check_vma=False
    )
```

```python
import functools

import jax
import jax.numpy as jnp
import numpy as np
from jax import lax
from jax.experimental import pallas as pl
from jax.experimental.pallas import tpu as pltpu
from jax.sharding import PartitionSpec as P

KVH = 4
HD = 128
SUB = 8
HUGE = 1e30
MESH = pl.DeviceIdType.MESH


def block_kernel(
    gy, gx_count, rows,
    lengths, inverse, x, gain, wq, wk, wv, wo, kc, vc,
    out,
    xall, ssq, wq_v, wk_v, wv_v, wo_v, kc_v, vc_v,
    part, kpart, vpart, part_in, qtile, qsend, qin, kvsend, kvin, qg,
    sums, box, box_in, stat, stat_in, att, osend, pin, oin,
    sem_wq, sem_wk, sem_wv, sem_wo, sem_kc, sem_vc,
    ssq_s, ssq_r, x_s, x_f, x_r, part_s, part_r, q_s, q_r, kv_s, kv_r,
    box_s, box_r, stat_s, stat_r, att_s, att_r, p_s, p_r, o_s, o_r,
):
    gx = lax.axis_index("gx")
    me = lax.axis_index("gy")
    other = 1 - gx
    half = gy // 2
    mate = me + 1 - 2 * (me % 2)
    bd = x.shape[1]
    qw = wq.shape[1]
    ck = wk.shape[0]
    span = kc.shape[1]
    ow = wo.shape[1] // gy
    hh = qw // HD
    hq = max(1, hh // KVH)
    nq = gy * hh // KVH
    bph = gy // KVH
    group = me // bph
    block = me % bph
    cj = ck // KVH
    qm = qsend.shape[1]
    d_model = bd * gy * gx_count

    def block_at(step):
        return (me + (step // half) * (mate - me) + 2 * (step % half)) % gy

    def load_in(step):
        base = pl.multiple_of(block_at(step) * bd, bd)
        rows_here = pl.ds(base, bd)
        return (
            pltpu.make_async_copy(wq.at[rows_here, :], wq_v.at[step], sem_wq.at[step]),
            pltpu.make_async_copy(wk.at[:, rows_here], wk_v.at[step], sem_wk.at[step]),
            pltpu.make_async_copy(wv.at[:, rows_here], wv_v.at[step], sem_wv.at[step]),
        )

    def load_out(step):
        first = mate + (step // half) * (me - mate)
        base = pl.multiple_of(((first + 2 * ((step + 1) % half)) % gy) * ow, ow)
        return pltpu.make_async_copy(wo.at[:, pl.ds(base, ow)], wo_v.at[step], sem_wo.at[step])

    def load_cache(row):
        return (
            pltpu.make_async_copy(kc.at[row], kc_v.at[row], sem_kc.at[row]),
            pltpu.make_async_copy(vc.at[row], vc_v.at[row], sem_vc.at[row]),
        )

    for step in range(gy):
        for copy in load_in(step):
            copy.start()

    barrier = pltpu.get_barrier_semaphore()
    for side in range(gx_count):
        for step in range(gy):
            if side == 0 and step == 0:
                continue
            pl.semaphore_signal(
                barrier, inc=1,
                device_id={"gx": (gx + side) % gx_count, "gy": (me + step) % gy},
                device_id_type=MESH,
            )

    own = x[...].astype(jnp.float32)
    mine = jnp.concatenate(
        [
            own[:rows], gain[...].astype(jnp.float32), jnp.zeros((SUB - rows - 1, bd), jnp.float32),
            own[rows:], jnp.zeros((SUB - rows, bd), jnp.float32),
        ],
        axis=0,
    )
    diagonal = lax.broadcasted_iota(jnp.int32, (2 * SUB, HD), 0) == lax.broadcasted_iota(
        jnp.int32, (2 * SUB, HD), 1
    )
    squares = jnp.sum(mine * mine, axis=1, keepdims=True)
    my_id = gx * gy + me
    ssq[my_id] = jnp.broadcast_to(
        jnp.sum(jnp.where(diagonal, squares, 0.0), axis=0, keepdims=True), (SUB, HD)
    )
    xall[me] = mine.astype(jnp.bfloat16)

    pl.semaphore_wait(barrier, gx_count * gy - 1)

    def ssq_copy(side, step, source):
        return pltpu.make_async_remote_copy(
            src_ref=ssq.at[my_id, pl.ds(0, 1)], dst_ref=ssq.at[source, pl.ds(0, 1)],
            send_sem=ssq_s.at[side, step], recv_sem=ssq_r.at[source],
            device_id={"gx": (gx + side) % gx_count, "gy": (me + step) % gy},
            device_id_type=MESH,
        )

    def peer_copy(src, dst, send, recv, step):
        return pltpu.make_async_remote_copy(
            src_ref=src, dst_ref=dst, send_sem=send, recv_sem=recv,
            device_id={"gy": (me + step) % gy}, device_id_type=MESH,
        )

    def core_copy(src, dst, send, recv):
        return pltpu.make_async_remote_copy(
            src_ref=src, dst_ref=dst, send_sem=send, recv_sem=recv,
            device_id={"gx": other}, device_id_type=MESH,
        )

    def gy_copy(src, dst, send, recv, device):
        return pltpu.make_async_remote_copy(
            src_ref=src, dst_ref=dst, send_sem=send, recv_sem=recv,
            device_id={"gy": device}, device_id_type=MESH,
        )

    def x_copy(k, source):
        device = mate if k == 0 else (me + 2 * k) % gy
        return gy_copy(xall.at[me], xall.at[source], x_s.at[k], x_r.at[source], device)

    def x_forward(k):
        passed = (me + 2 * k) % gy
        return gy_copy(xall.at[passed], xall.at[passed], x_f.at[k], x_r.at[passed], mate)

    def x_wait(source):
        gy_copy(xall.at[me], xall.at[source], x_s.at[0], x_r.at[source], mate).wait_recv()

    for side in range(gx_count):
        for step in range(gy):
            if side or step:
                ssq_copy(side, step, my_id).start()
    for k in list(range(1, half)) + [0]:
        x_copy(k, me).start()
    for row in range(rows):
        for copy in load_cache(row):
            copy.start()

    part[...] = jnp.zeros_like(part)
    kpart[...] = jnp.zeros_like(kpart)
    vpart[...] = jnp.zeros_like(vpart)
    row_of = lax.broadcasted_iota(jnp.int32, (SUB, HD), 0)
    lens = jnp.zeros((SUB, HD), jnp.int32)
    for row in range(rows):
        lens = jnp.where(row_of == row, lengths[row], lens)
    lens = lens.astype(jnp.float32)
    angles = lens * inverse[...]
    cosine = jnp.cos(angles)
    sine = jnp.sin(angles)
    sine = jnp.where(lax.broadcasted_iota(jnp.int32, (SUB, HD), 1) < HD // 2, -sine, sine)
    sums[...] = jnp.zeros_like(sums)
    qtile[...] = jnp.zeros_like(qtile)
    for k in range(1, half):
        x_wait((me + 2 * k) % gy)
        x_forward(k).start()

    for side in range(gx_count):
        for step in range(gy):
            if side or step:
                source = ((gx + side) % gx_count) * gy + (me + step) % gy
                ssq_copy(side, step, source).wait_recv()
    total = jnp.sum(ssq[:, 0, :], axis=0, keepdims=True)
    total = jnp.sum(jnp.where(diagonal, total, 0.0), axis=1, keepdims=True)
    scale_inv = lax.rsqrt(total / d_model + 1e-05)

    def project(step):
        features = xall[block_at(step)].astype(jnp.float32)
        gain = features[rows : rows + 1, :]
        normed = (features * scale_inv * gain).astype(jnp.bfloat16)
        for copy in load_in(step):
            copy.wait()
        query = jnp.dot(normed, wq_v[step], preferred_element_type=jnp.float32)
        part[0, :, :qw] += query[:SUB]
        part[1, :, :qw] += query[SUB:]
        across = (((1,), (1,)), ((), ()))
        kpart[...] += lax.dot_general(
            normed, wk_v[step], across, preferred_element_type=jnp.float32
        )
        vpart[...] += lax.dot_general(
            normed, wv_v[step], across, preferred_element_type=jnp.float32
        )

    @pl.loop(0, half)
    def _(step):
        project(step)

    @pl.loop(half, gy)
    def _(step):
        x_wait(block_at(step))
        project(step)

    for side in range(2):
        part[side, :, qw : qw + ck] = kpart[side * SUB : (side + 1) * SUB]
        part[side, :, qw + HD : qw + HD + ck] = vpart[side * SUB : (side + 1) * SUB]

    swap = core_copy(part.at[other], part_in, part_s, part_r)
    swap.start()
    for step in range(gy):
        load_out(step).start()
    column = lax.broadcasted_iota(jnp.int32, (HD, KVH * HD), 0)
    target = lax.broadcasted_iota(jnp.int32, (HD, KVH * HD), 1)
    wanted = (target % HD) * KVH + target // HD
    select = jnp.where((column < ck) & (column == wanted), 1.0, 0.0).astype(jnp.bfloat16)
    swap.wait_recv()

    def rotated(values):
        return values * cosine + pltpu.roll(values, HD // 2, 1) * sine

    summed = part[gx] + part_in[...]
    for slot in range(hh):
        turned = rotated(summed[:, slot * HD : (slot + 1) * HD])
        to_group = slot % KVH if hh % KVH == 0 else (me * hh + slot) % KVH
        at = slot // KVH * SUB
        qtile[to_group, at : at + SUB] = turned
    qsend[...] = qtile[...].astype(jnp.bfloat16)
    pair = jnp.concatenate([summed[:, qw : qw + HD], summed[:, qw + HD :]], axis=0)
    high = pair.astype(jnp.bfloat16)
    rest = pair - high.astype(jnp.float32)
    middle = rest.astype(jnp.bfloat16)
    low = (rest - middle.astype(jnp.float32)).astype(jnp.bfloat16)
    placed = (
        jnp.dot(high, select, preferred_element_type=jnp.float32)
        + jnp.dot(middle, select, preferred_element_type=jnp.float32)
        + jnp.dot(low, select, preferred_element_type=jnp.float32)
    )
    for g in range(KVH):
        lanes = slice(g * HD, (g + 1) * HD)
        kvsend[g] = placed[:SUB, lanes] + pltpu.roll(placed[SUB:, lanes], HD // 2, 1)

    def q_copies(step, source):
        to_group = ((me + step) % gy) // bph
        return (
            peer_copy(qsend.at[to_group], qin.at[source], q_s.at[step], q_r.at[source], step),
            peer_copy(kvsend.at[to_group], kvin.at[source], kv_s.at[step], kv_r.at[source], step),
        )

    for step in range(1, gy):
        for copy in q_copies(step, me):
            copy.start()
    qin[me] = qsend[group]
    kvin[me] = kvsend[group]
    for step in range(1, gy):
        for copy in q_copies(step, (me + step) % gy):
            copy.wait_recv()

    if hh % KVH == 0:
        for source in range(gy):
            tile = qin[source].astype(jnp.float32)
            for slot in range(hq):
                qg[source * hq + slot] = tile[slot * SUB : (slot + 1) * SUB]
    else:
        for n in range(nq):
            qg[n] = qin[(n * KVH + group) // hh].astype(jnp.float32)[:SUB]
    lane8 = lax.broadcasted_iota(jnp.int32, (SUB, HD), 1)
    own_key = jnp.zeros((SUB, HD), jnp.float32)
    own_value = jnp.zeros((SUB, HD), jnp.float32)
    for source in range(gy):
        tile = kvin[source]
        key_lanes = jnp.where(lane8 < HD // 2, tile, 0.0)
        value_lanes = jnp.where(lane8 < HD // 2, 0.0, tile)
        own_key += pltpu.roll(key_lanes, source * cj, 1) if source else key_lanes
        own_value += pltpu.roll(value_lanes, (source * cj + HD // 2) % HD, 1)
    own_key = rotated(own_key).astype(jnp.bfloat16).astype(jnp.float32)
    own_value = own_value.astype(jnp.bfloat16).astype(jnp.float32)

    score_scale = HD ** (-0.5)
    with_self = (lax.broadcasted_iota(jnp.int32, (nq, 1), 0) * 0 + block) == 0
    positions = (lax.broadcasted_iota(jnp.int32, (nq, span), 1) + block * span).astype(jnp.float32)
    lane = lax.broadcasted_iota(jnp.int32, (nq, HD), 1)
    stats = jnp.zeros((nq, HD), jnp.float32)
    for row in range(rows):
        for copy in load_cache(row):
            copy.wait()
        query = qg[:, row, :]
        scores = (
            lax.dot_general(
                query.astype(jnp.bfloat16), kc_v[row], (((1,), (1,)), ((), ())),
                preferred_element_type=jnp.float32,
            )
            * score_scale
        )
        live = positions < lens[row : row + 1, 0:1]
        masked = jnp.where(live, scores, -HUGE)
        self_score = (
            jnp.sum(query * own_key[row : row + 1, :], axis=1, keepdims=True) * score_scale
        )
        self_live = jnp.where(with_self, self_score, -HUGE)
        best = jnp.maximum(jnp.max(masked, axis=1, keepdims=True), self_live)
        weights = jnp.where(live, jnp.exp(masked - best), 0.0)
        self_weight = jnp.where(with_self, jnp.exp(self_live - best), 0.0)
        denominator = jnp.sum(weights, axis=1, keepdims=True) + self_weight
        weighted = jnp.dot(
            weights.astype(jnp.bfloat16), vc_v[row], preferred_element_type=jnp.float32
        )
        weighted = (
            weighted
            + self_weight.astype(jnp.bfloat16).astype(jnp.float32) * own_value[row : row + 1, :]
        )
        sums[:, row, :] = weighted
        stats = jnp.where(lane == row, best, stats)
        stats = jnp.where(lane == SUB + row, denominator, stats)

    stat[...] = jnp.zeros_like(stat)
    for owner in range(gy):
        first = owner * hh // KVH
        heads = [sums[first + slot] for slot in range(hq)]
        heads += [jnp.zeros((SUB, HD), jnp.float32)] * (qm // SUB - hq)
        box[owner] = jnp.concatenate(heads, axis=0).astype(jnp.bfloat16)
        stat[owner, :hq] = stats[first : first + hq]

    def box_copies(step, source):
        owner = (me + step) % gy
        return (
            peer_copy(
                stat.at[owner, pl.ds(0, hq)], stat_in.at[source, pl.ds(0, hq)],
                stat_s.at[step], stat_r.at[source], step,
            ),
            peer_copy(box.at[owner], box_in.at[source], box_s.at[step], box_r.at[source], step),
        )

    for step in range(1, gy):
        for copy in box_copies(step, me):
            copy.start()
    box_in[me] = box[me]
    stat_in[me] = stat[me]
    for step in range(1, gy):
        for copy in box_copies(step, (me + step) % gy):
            copy.wait_recv()

    for slot in range(hh):
        of_group = slot % KVH if hh % KVH == 0 else (me * hh + slot) % KVH
        at = slot // KVH
        bests, denominators, parts = [], [], []
        for b in range(bph):
            source = of_group * bph + b
            line = stat_in[source, at : at + 1, :]
            bests.append(jnp.sum(jnp.where(lane8 == row_of, line, 0.0), axis=1, keepdims=True))
            denominators.append(
                jnp.sum(jnp.where(lane8 == row_of + SUB, line, 0.0), axis=1, keepdims=True)
            )
            parts.append(box_in[source].astype(jnp.float32)[at * SUB : (at + 1) * SUB])
        overall = functools.reduce(jnp.maximum, bests)
        factors = [jnp.exp(best - overall) for best in bests]
        denominator = sum(f * d for f, d in zip(factors, denominators))
        weighted = sum(f * p for f, p in zip(factors, parts))
        att[gx, :, slot * HD : (slot + 1) * HD] = (
            (weighted / denominator).astype(jnp.bfloat16).astype(jnp.float32)
        )

    att_swap = core_copy(att.at[gx], att.at[gx], att_s, att_r)
    att_swap.start()
    core_copy(att.at[other], att.at[other], att_s, att_r).wait_recv()
    attended = jnp.concatenate([att[0], att[1]], axis=0).astype(jnp.bfloat16)

    def p_copy(k):
        return gy_copy(osend.at[k], pin.at[k], p_s.at[k], p_r.at[k], mate)

    def o_copy(k, source):
        return gy_copy(
            osend.at[half + k], oin.at[source // 2], o_s.at[k], o_r.at[source // 2],
            (me + 2 * k) % gy,
        )

    @pl.loop(0, half)
    def _(step):
        k = (step + 1) % half
        load_out(step).wait()
        osend[k] = jnp.dot(
            attended, wo_v[step], preferred_element_type=jnp.float32
        ).astype(jnp.bfloat16)
        p_copy(k).start()

    @pl.loop(half, gy - 1)
    def _(step):
        k = step + 1 - half
        load_out(step).wait()
        share = jnp.dot(attended, wo_v[step], preferred_element_type=jnp.float32)
        p_copy(k).wait_recv()
        osend[half + k] = (share + pin[k].astype(jnp.float32)).astype(jnp.bfloat16)
        o_copy(k, me).start()

    load_out(gy - 1).wait()
    result = jnp.dot(attended, wo_v[gy - 1], preferred_element_type=jnp.float32)
    p_copy(0).wait_recv()
    result = result + pin[0].astype(jnp.float32)
    for k in range(1, half):
        source = (me + 2 * k) % gy
        o_copy(k, source).wait_recv()
        result = result + oin[source // 2].astype(jnp.float32)
    out[...] = jnp.concatenate([result[:rows], result[SUB : SUB + rows]], axis=0).astype(out.dtype)

    swap.wait_send()
    att_swap.wait_send()
    for side in range(gx_count):
        for step in range(gy):
            if side or step:
                ssq_copy(side, step, my_id).wait_send()
    for k in range(half):
        x_copy(k, me).wait_send()
        p_copy(k).wait_send()
        if k:
            x_forward(k).wait_send()
            o_copy(k, me).wait_send()
    for step in range(1, gy):
        for copy in q_copies(step, me) + box_copies(step, me):
            copy.wait_send()


def local(inputs, norm_gain, w_query, w_key, w_value, w_out, key_cache, value_cache, lengths):
    gy, gx_count = lax.axis_size("gy"), lax.axis_size("gx")
    rows, span, _ = key_cache.shape
    bd = inputs.shape[1]
    qw, ck = w_query.shape[1], w_key.shape[1]
    ow = w_out.shape[1] // gy
    hh = qw // HD
    hq = max(1, hh // KVH)
    nq = gy * hh // KVH
    half = gy // 2
    qm = max(2 * SUB, hq * SUB)
    bf16, f32 = jnp.bfloat16, jnp.float32

    half_dim = HD // 2
    inverse = 500000.0 ** (-2.0 * np.arange(half_dim, dtype=np.float64) / HD)
    inverse = jnp.asarray(np.tile(inverse, 2)[None, :], f32)

    vmem = pl.BlockSpec(memory_space=pltpu.VMEM)
    hbm = pl.BlockSpec(memory_space=pl.ANY)
    dma = pltpu.SemaphoreType.DMA
    scratch = [
        pltpu.VMEM((gy, 2 * SUB, bd), bf16),
        pltpu.VMEM((gx_count * gy, SUB, HD), f32),
        pltpu.VMEM((gy, bd, qw), bf16),
        pltpu.VMEM((gy, ck, bd), bf16),
        pltpu.VMEM((gy, ck, bd), bf16),
        pltpu.VMEM((gy, w_out.shape[0], ow), bf16),
        pltpu.VMEM(key_cache.shape, bf16),
        pltpu.VMEM(value_cache.shape, bf16),
        pltpu.VMEM((2, SUB, qw + 2 * HD), f32),
        pltpu.VMEM((2 * SUB, ck), f32),
        pltpu.VMEM((2 * SUB, ck), f32),
        pltpu.VMEM((SUB, qw + 2 * HD), f32),
        pltpu.VMEM((KVH, qm, HD), f32),
        pltpu.VMEM((KVH, qm, HD), bf16),
        pltpu.VMEM((gy, qm, HD), bf16),
        pltpu.VMEM((KVH, SUB, HD), f32),
        pltpu.VMEM((gy, SUB, HD), f32),
        pltpu.VMEM((nq, SUB, HD), f32),
        pltpu.VMEM((nq, SUB, HD), f32),
        pltpu.VMEM((gy, qm, HD), bf16),
        pltpu.VMEM((gy, qm, HD), bf16),
        pltpu.VMEM((gy, SUB, HD), f32),
        pltpu.VMEM((gy, SUB, HD), f32),
        pltpu.VMEM((2, SUB, qw), f32),
        pltpu.VMEM((gy, 2 * SUB, ow), bf16),
        pltpu.VMEM((half, 2 * SUB, ow), bf16),
        pltpu.VMEM((half, 2 * SUB, ow), bf16),
        dma((gy,)), dma((gy,)), dma((gy,)), dma((gy,)), dma((rows,)), dma((rows,)),
        dma((gx_count, gy)), dma((gx_count * gy,)),
        dma((half,)), dma((half,)), dma((gy,)),
        dma, dma,
        dma((gy,)), dma((gy,)), dma((gy,)), dma((gy,)),
        dma((gy,)), dma((gy,)), dma((gy,)), dma((gy,)),
        dma, dma,
        dma((half,)), dma((half,)), dma((half,)), dma((half,)),
    ]
    return pl.pallas_call(
        functools.partial(block_kernel, gy, gx_count, rows),
        out_shape=jax.ShapeDtypeStruct((2 * rows, ow), bf16),
        in_specs=[pl.BlockSpec(memory_space=pltpu.SMEM)] + [vmem] * 3 + [hbm] * 6,
        out_specs=vmem,
        scratch_shapes=scratch,
        compiler_params=pltpu.CompilerParams(
            collective_id=0, has_side_effects=True, vmem_limit_bytes=60 * 2**20
        ),
    )(
        lengths, inverse, inputs, norm_gain[None, :],
        w_query, w_key.T, w_value.T, w_out, key_cache, value_cache,
    )


def solution(mesh):
    placed = (
        P("groups", ("gx", "gy")),
        P(("gx", "gy")),
        P("gx", "gy"),
        P("gx", "gy"),
        P("gx", "gy"),
        P("gy", "gx"),
        P(("groups", "gx"), "gy", None),
        P(("groups", "gx"), "gy", None),
        P(("groups", "gx")),
    )
    return jax.shard_map(
        local, mesh=mesh, in_specs=placed, out_specs=P("groups", ("gx", "gy")), check_vma=False
    )
```
